256 devices in a mesh: learn: 8 (over z_lo, x), expert: 32 (over z_hi, y, core).
Axes of the slice: x: 4, y: 4, z: 8 (z_hi: 4, z_lo: 2; z = z_hi * 2 + z_lo), core: 2. Of those that a mesh axis runs over, the one named last changes fastest.
Arguments:
- update: float32 [32, 160, 128, 128], P('learn', 'expert'), may hold values from -3 to 3
- resident: bfloat16 [32, 2560, 1024], P('expert'), may hold values from -6 to 6
- placement: int32 [32], replicated, may hold values from 0 to 31, each once
- counts: int32 [32], replicated, may hold values from 1 to 160, as said below
Outputs:
- refreshed: bfloat16 [32, 2560, 1024], P('expert')
The draws below stay inside these ranges and needn't reach their ends.
Inputs may be any that keep to these rules, and one draw needn't show every extreme that they name: `counts`: some expert changes all 160 blocks and another exactly one.
All inputs are finite; a program needn't handle non-finite values.
Results may differ from the reference program's by a relative error of at most 0.0034.
Values may be sent and summed in bfloat16 or wider, within the bound.
A program may use at most 128 MiB of HBM per device.

```python
import math
import jax
import jax.numpy as jnp
from jax import lax

D_WIN = 2560
H_WIN = 1024
TILE = 128
TILE_ROWS = 20
TILE_COLS = 8
TILES_EXP = 160
EXPERTS = 32


def draw_update(key, part):
    key = jax.random.fold_in(key, 5)
    first, second = jax.random.split(key)
    shape = (EXPERTS, TILES_EXP, TILE, TILE)
    values = jnp.clip(jax.random.normal(first, shape, jnp.float32), -6.0, 6.0)
    spread = jax.random.uniform(second, (EXPERTS, TILES_EXP, 1, 1), jnp.float32, math.log(0.05), math.log(0.5))
    return values * jnp.exp(spread)


def draw_counts(key, part):
    key = jax.random.fold_in(key, 11)
    first, second = jax.random.split(key)
    base = jax.random.randint(first, (EXPERTS,), 1, TILES_EXP + 1)
    chosen = jax.random.randint(second, (), 0, EXPERTS)
    expert_ids = jnp.arange(EXPERTS)
    base = jnp.where(expert_ids == chosen, TILES_EXP, base)
    base = jnp.where(expert_ids == (chosen + 1) % EXPERTS, 1, base)
    return base.astype(jnp.int32)


def steps_of(rng, shape, shards, least, top_value):
    factor_of = 1.0
    for position, parts in shards:
        heights = jax.random.uniform(jax.random.fold_in(jax.random.fold_in(rng, 6), position), (parts,), jnp.float32, least / len(shards), top_value / len(shards))
        factor_of = factor_of * jnp.repeat(jnp.exp(heights), shape[position] // parts).reshape((-1,) + (1,) * (len(shape) - 1 - position))
    return factor_of


def noise(stream_key, dims, deviation, bound, cuts=(), held_as=jnp.bfloat16):
    result = deviation * jax.random.normal(stream_key, dims, jnp.float32)
    if cuts:
        result = result * steps_of(stream_key, dims, cuts, -0.22, 0.18)
    return jnp.clip(result, -bound, bound).astype(held_as)


def setup_inputs(seed: int = 0) -> dict:
    keys = jax.random.split(jax.random.key(seed), 5)
    update = draw_update(jax.random.fold_in(keys[4], 71), 0)
    resident = noise(keys[1], (EXPERTS, D_WIN, H_WIN), 1.0, 6.0, ((0, 32),))
    placement = jax.random.permutation(keys[2], EXPERTS).astype(jnp.int32)
    counts = draw_counts(jax.random.fold_in(keys[4], 71), 0)
    return dict(update=update, resident=resident, placement=placement, counts=counts)


def reference(update, resident, placement, counts):
    largest = jnp.max(jnp.abs(update), axis=(2, 3))
    block_scale = ((largest + 1e-6) / 448.0).astype(jnp.bfloat16)
    scale_full = block_scale.astype(jnp.float32)
    code_tiles = (update / scale_full[:, :, None, None]).astype(jnp.bfloat16)
    slot_ids = jnp.arange(EXPERTS, dtype=jnp.int32)
    expert_ids = jnp.arange(EXPERTS, dtype=jnp.int32)
    owner_expert = jnp.sum(jnp.where(placement[None, :] == slot_ids[:, None], expert_ids[None, :], 0), axis=1).astype(jnp.int32)
    tile_ids = jnp.arange(TILES_EXP, dtype=jnp.int32)

    def refresh(pair):
        expert, current = pair
        changed = (tile_ids < counts[expert]).astype(jnp.float32)
        decoded = code_tiles[expert].astype(jnp.float32) * (scale_full[expert] * changed)[:, None, None]
        window = decoded.reshape(TILE_ROWS, TILE_COLS, TILE, TILE).transpose(0, 2, 1, 3).reshape(D_WIN, H_WIN)
        return (current.astype(jnp.float32) + window).astype(jnp.bfloat16)

    return lax.map(refresh, (owner_expert, resident))
```

```python
import jax
import jax.numpy as jnp
from jax import lax
from jax.experimental import pallas as pl
from jax.experimental.pallas import tpu as pltpu
from jax.sharding import PartitionSpec as P

MESH = pl.DeviceIdType.MESH
NX, NZ, NH, NY, NC = 4, 2, 4, 4, 2
NL, NE = 8, 32
EXP, PER, TPD = 4, 8, 5
SLAB, LANE = 16, 128
BLK = 40
ROW_TILES = 5


def kernel(update, resident, placement, counts, out,
           upd, res, acc, s1, r1, s2, gat, owner,
           upd_sem, res_sem, out_sem, s1_send, s1_recv, s2_send, s2_recv,
           g_send, g_recv):
    l = lax.axis_index("learn")
    e = lax.axis_index("expert")
    zl, x = l // NX, l % NX
    zh, y, c = e // (NY * NC), (e // NC) % NY, e % NC
    right = (zl * NX + (x + 1) % NX, e)
    left = (zl * NX + (x + 3) % NX, e)
    across = ((1 - zl) * NX + x, e)

    upd_in = pltpu.make_async_copy(update, upd, upd_sem)
    upd_in.start()
    res_in = pltpu.make_async_copy(resident, res, res_sem)
    res_in.start()

    learn_peers = [(((zl + dz) % NZ) * NX + (x + dx) % NX) for dz in range(NZ) for dx in range(NX) if (dz, dx) != (0, 0)]

    def slot(dh, dy, dc):
        return ((zh + dh) % NH) * (NY * NC) + ((y + dy) % NY) * NC + (c + dc) % NC

    near = [slot(0, dy, dc) for dy in range(NY) for dc in range(NC) if (dy, dc) != (0, 0)]
    far = {dh: [slot(dh, dy, dc) for dy in range(NY) for dc in range(NC)] for dh in (1, 3, 2)}
    expert_peers = near + far[1] + far[3] + far[2]

    barrier = pltpu.get_barrier_semaphore()
    for peer in learn_peers:
        pl.semaphore_signal(barrier, inc=1, device_id=(peer, e), device_id_type=MESH)
    for peer in expert_peers:
        pl.semaphore_signal(barrier, inc=1, device_id=(l, peer), device_id_type=MESH)

    upd_in.wait()

    def encode(t, carry):
        i = t // TPD
        j = t % TPD
        u = upd[t]
        largest = jnp.max(jnp.abs(u), axis=(0, 1), keepdims=True)
        scale = ((largest + 1e-06) / 448.0).astype(jnp.bfloat16).astype(jnp.float32)
        code = (u / scale).astype(jnp.bfloat16).astype(jnp.float32)
        changed = jnp.where(e * TPD + j < counts[l * EXP + i], 1.0, 0.0).astype(jnp.float32)
        s1[:, t] = (code * (scale * changed)).astype(jnp.bfloat16).reshape(NL, SLAB, LANE)
        return carry

    lax.fori_loop(0, EXP * TPD, encode, 0)
    pl.semaphore_wait(barrier, len(learn_peers) + len(expert_peers))

    sends1 = []
    for n, peer in enumerate(learn_peers):
        cp = pltpu.make_async_remote_copy(
            src_ref=s1.at[peer], dst_ref=r1.at[l], send_sem=s1_send.at[n], recv_sem=s1_recv.at[l],
            device_id=(peer, e), device_id_type=MESH)
        cp.start()
        sends1.append(cp)
    r1[l] = s1[l]

    def owner_of(k, carry):
        def add(n, total):
            return jnp.maximum(total, jnp.where(placement[n] == k, n, 0))
        owner[k] = lax.fori_loop(0, NE, add, 0, unroll=True)
        return carry

    lax.fori_loop(0, NE, owner_of, 0)

    def recv1(peer):
        return pltpu.make_async_remote_copy(
            src_ref=r1.at[peer], dst_ref=r1.at[peer], send_sem=s1_send.at[0], recv_sem=s1_recv.at[peer],
            device_id=(peer, e), device_id_type=MESH)

    for peer in learn_peers:
        recv1(peer).wait_recv()

    def picked(k):
        o = owner[k]
        return r1[o // EXP, pl.ds((o % EXP) * TPD, TPD)]

    sends2 = []
    for n, k in enumerate(expert_peers):
        s2[n] = picked(k)
        cp = pltpu.make_async_remote_copy(
            src_ref=s2.at[n], dst_ref=gat.at[l, zh, pl.ds((y * NC + c) * TPD, TPD)],
            send_sem=s2_send.at[n], recv_sem=s2_recv.at[e],
            device_id=(l, k), device_id_type=MESH)
        cp.start()
        sends2.append(cp)
    gat[l, zh, pl.ds((y * NC + c) * TPD, TPD)] = picked(e)

    def recv2(k):
        ref = gat.at[l, k // (NY * NC), pl.ds((k % (NY * NC)) * TPD, TPD)]
        pltpu.make_async_remote_copy(
            src_ref=ref, dst_ref=ref, send_sem=s2_send.at[0], recv_sem=s2_recv.at[k],
            device_id=(l, k), device_id_type=MESH).wait_recv()

    sends3 = []

    def plane(dz, dx):
        return ((zl + dz) % NZ) * NX + (x + dx) % NX

    def part(src, q, half):
        if half is None:
            return gat.at[src, q]
        return gat.at[src, q, pl.ds(half * (BLK // 2), BLK // 2)]

    def push(src, q, to, half=None):
        ref = part(src, q, half)
        cp = pltpu.make_async_remote_copy(
            src_ref=ref, dst_ref=ref, send_sem=g_send.at[len(sends3)], recv_sem=g_recv.at[src, q, 0 if half is None else half],
            device_id=to, device_id_type=MESH)
        cp.start()
        sends3.append(cp)

    def arrive(src, q, half=None):
        ref = part(src, q, half)
        pltpu.make_async_remote_copy(
            src_ref=ref, dst_ref=ref, send_sem=g_send.at[0], recv_sem=g_recv.at[src, q, 0 if half is None else half],
            device_id=across, device_id_type=MESH).wait_recv()

    def add(src, q):
        def row(a, carry):
            at = pl.multiple_of((q * ROW_TILES + a) * LANE + src * SLAB, SLAB)
            for b in range(8):
                cols = pl.ds(b * LANE, LANE)
                acc[pl.ds(at, SLAB), cols] = (
                    res[pl.ds(at, SLAB), cols].astype(jnp.float32) + gat[src, q, a * 8 + b].astype(jnp.float32)
                ).astype(jnp.bfloat16)
            return carry
        lax.fori_loop(0, ROW_TILES, row, 0)

    chunk = {dh: (zh + dh) % NH for dh in range(NH)}
    own = plane(0, 0)

    for k in near:
        recv2(k)
    q0 = chunk[0]
    push(own, q0, right)
    push(own, q0, left)
    res_in.wait()
    add(own, q0)
    arrive(plane(0, 3), q0)
    push(plane(0, 3), q0, right, 0)
    arrive(plane(0, 1), q0)
    push(plane(0, 1), q0, left, 1)
    add(plane(0, 3), q0)
    add(plane(0, 1), q0)

    rest = (1, 3, 2)
    for dh in rest:
        q = chunk[dh]
        for k in far[dh]:
            recv2(k)
        push(own, q, across)
        push(own, q, right)
        push(own, q, left)
        add(own, q)
    arrive(plane(0, 2), q0, 0)
    arrive(plane(0, 2), q0, 1)
    add(plane(0, 2), q0)
    for dx in range(NX):
        push(plane(0, dx), q0, across)
    for dh in rest:
        q = chunk[dh]
        arrive(plane(0, 3), q)
        push(plane(0, 3), q, right, 0)
        arrive(plane(0, 1), q)
        push(plane(0, 1), q, left, 1)
        arrive(plane(1, 0), q)
        push(plane(1, 0), q, right)
        push(plane(1, 0), q, left)
        add(plane(0, 3), q)
        add(plane(0, 1), q)
        add(plane(1, 0), q)
    for dh in rest:
        q = chunk[dh]
        arrive(plane(0, 2), q, 0)
        arrive(plane(0, 2), q, 1)
        add(plane(0, 2), q)
        arrive(plane(1, 3), q)
        push(plane(1, 3), q, right, 0)
        arrive(plane(1, 1), q)
        push(plane(1, 1), q, left, 1)
        add(plane(1, 3), q)
        add(plane(1, 1), q)
    outs = []

    def store(q):
        rows = pl.ds(pl.multiple_of(q * (ROW_TILES * LANE), LANE), ROW_TILES * LANE)
        cp = pltpu.make_async_copy(acc.at[rows], out.at[rows], out_sem.at[len(outs)])
        cp.start()
        outs.append(cp)

    for dx in range(NX):
        arrive(plane(1, dx), q0)
        add(plane(1, dx), q0)
    store(q0)
    for dh in rest:
        q = chunk[dh]
        arrive(plane(1, 2), q, 0)
        arrive(plane(1, 2), q, 1)
        add(plane(1, 2), q)
        store(q)
    for cp in sends1 + sends2 + sends3:
        cp.wait_send()
    for cp in outs:
        cp.wait()


N_SENDS3 = 2 + 2 + 4 + 3 * (3 + 2 + 2 + 2)


def on_device(update, resident, placement, counts):
    _, rows, cols = resident.shape
    bf16 = jnp.bfloat16
    result = pl.pallas_call(
        kernel,
        out_shape=jax.ShapeDtypeStruct((rows, cols), bf16),
        in_specs=[
            pl.BlockSpec(memory_space=pl.ANY),
            pl.BlockSpec(memory_space=pl.ANY),
            pl.BlockSpec(memory_space=pltpu.SMEM),
            pl.BlockSpec(memory_space=pltpu.SMEM),
        ],
        out_specs=pl.BlockSpec(memory_space=pl.ANY),
        scratch_shapes=[
            pltpu.VMEM((EXP * TPD, LANE, LANE), jnp.float32),
            pltpu.VMEM((rows, cols), bf16),
            pltpu.VMEM((rows, cols), bf16),
            pltpu.VMEM((NL, EXP * TPD, SLAB, LANE), bf16),
            pltpu.VMEM((NL, EXP * TPD, SLAB, LANE), bf16),
            pltpu.VMEM((NE - 1, TPD, SLAB, LANE), bf16),
            pltpu.VMEM((NL, NH, BLK, SLAB, LANE), bf16),
            pltpu.SMEM((NE,), jnp.int32),
            pltpu.SemaphoreType.DMA,
            pltpu.SemaphoreType.DMA,
            pltpu.SemaphoreType.DMA((NH,)),
            pltpu.SemaphoreType.DMA((NL - 1,)),
            pltpu.SemaphoreType.DMA((NL,)),
            pltpu.SemaphoreType.DMA((NE - 1,)),
            pltpu.SemaphoreType.DMA((NE,)),
            pltpu.SemaphoreType.DMA((N_SENDS3,)),
            pltpu.SemaphoreType.DMA((NL, NH, 2)),
        ],
        compiler_params=pltpu.CompilerParams(collective_id=0, has_side_effects=True, vmem_limit_bytes=40 << 20),
        name="refresh",
    )(update.reshape(EXP * TPD, LANE, LANE), resident.reshape(rows, cols), placement, counts)
    return result[None]


def solution(mesh):
    placed = (P("learn", "expert", None, None), P("expert", None, None), P(), P())
    return jax.shard_map(
        on_device, mesh=mesh, in_specs=placed, out_specs=P("expert", None, None), check_vma=False
    )
```

```python
import jax
import jax.numpy as jnp
from jax import lax
from jax.experimental import pallas as pl
from jax.experimental.pallas import tpu as pltpu
from jax.sharding import PartitionSpec as P

MESH = pl.DeviceIdType.MESH
NX, NZ, NH, NY, NC = 4, 2, 4, 4, 2
NL, NE = 8, 32
EXP, PER, TPD = 4, 8, 5
SLAB, LANE = 16, 128
BLK = 40
SIDE = NY * NC
VMEM_LIMIT = 48 << 20
ROW_TILES = 5


def kernel(update, resident, placement_in, counts_in, out,
           upd, res, s1, r1, s2, gat, placement, counts, owner,
           in_sem, s1_send, s1_recv, s2_send, s2_recv, g_send, g_recv):
    l = lax.axis_index("learn")
    e = lax.axis_index("expert")
    zl, x = l // NX, l % NX
    zh, y, c = e // (NY * NC), (e // NC) % NY, e % NC
    right = (zl * NX + (x + 1) % NX, e)
    left = (zl * NX + (x + 3) % NX, e)
    across = ((1 - zl) * NX + x, e)

    ins = []
    for n, (src, dst) in enumerate(((counts_in, counts), (update, upd), (placement_in, placement), (resident, res))):
        cp = pltpu.make_async_copy(src, dst, in_sem.at[n])
        cp.start()
        ins.append(cp)
    counts_ready, upd_ready, placement_ready, res_ready = ins

    learn_peers = [(((zl + dz) % NZ) * NX + (x + dx) % NX) for dz in range(NZ) for dx in range(NX) if (dz, dx) != (0, 0)]

    def slot(dh, n):
        return ((zh + dh) % NH) * SIDE + (((y + n // NC) % NY) * NC + (c + n) % NC)

    def zl_at(dh):
        return {0: zl, 1: 0, 3: 1, 2: 1 - zl}[dh]

    def sources(dh):
        back = (4 - dh) % NH
        if dh == 0:
            return [(zl, slot(0, n)) for n in range(1, SIDE)]
        if dh == 2:
            return [(1 - zl, slot(2, n)) for n in range(SIDE)]
        at = (zh + 3 + 2 * zl) % NH
        source_zl = zl if dh == 1 else 1 - zl
        return [(source_zl, at * SIDE + slot(0, n) % SIDE) for n in range(SIDE)]

    targets = {dh: [(zl_at(dh) * NX + x, slot(dh, n)) for n in range(1 if dh == 0 else 0, SIDE)] for dh in (0, 1, 3, 2)}

    barrier = pltpu.get_barrier_semaphore()
    for peer in learn_peers:
        pl.semaphore_signal(barrier, inc=1, device_id=(peer, e), device_id_type=MESH)
    for dh in (0, 1, 3, 2):
        for source_zl, k in sources(dh):
            pl.semaphore_signal(barrier, inc=1, device_id=(source_zl * NX + x, k), device_id_type=MESH)

    counts_ready.wait()
    upd_ready.wait()

    def encode(t, carry):
        u = upd[t]
        largest = jnp.max(jnp.abs(u), axis=(0, 1), keepdims=True)
        scale = ((largest + 1e-06) / 448.0).astype(jnp.bfloat16).astype(jnp.float32)
        code = (u * (1.0 / scale)).astype(jnp.bfloat16).astype(jnp.float32)
        changed = jnp.where(e * TPD + t % TPD < counts[l * EXP + t // TPD], 1.0, 0.0).astype(jnp.float32)
        s1[:, t] = (code * (scale * changed)).astype(jnp.bfloat16).reshape(NL, SLAB, LANE)
        return carry

    lax.fori_loop(0, EXP * TPD, encode, 0, unroll=5)
    pl.semaphore_wait(barrier, NL - 1 + NE - 1)

    sends = []
    for n, peer in enumerate(learn_peers):
        cp = pltpu.make_async_remote_copy(
            src_ref=s1.at[peer], dst_ref=r1.at[l], send_sem=s1_send.at[n], recv_sem=s1_recv.at[l],
            device_id=(peer, e), device_id_type=MESH)
        cp.start()
        sends.append(cp)
    r1[l] = s1[l]
    placement_ready.wait()

    def owner_of(k, carry):
        def step(n, best):
            return jnp.maximum(best, jnp.where(placement[n] == k, n, 0))
        owner[k] = lax.fori_loop(0, NE, step, 0, unroll=True)
        return carry

    lax.fori_loop(0, NE, owner_of, 0)
    res_ready.wait()
    for peer in learn_peers:
        pltpu.make_async_remote_copy(
            src_ref=r1.at[peer], dst_ref=r1.at[peer], send_sem=s1_send.at[0], recv_sem=s1_recv.at[peer],
            device_id=(peer, e), device_id_type=MESH).wait_recv()

    mine = pl.ds((y * NC + c) * TPD, TPD)

    def picked(k):
        o = owner[k]
        return r1[o // EXP, pl.ds((o % EXP) * TPD, TPD)]

    sent = [0]

    def send_to(dh):
        for peer, k in targets[dh]:
            n = sent[0]
            sent[0] += 1
            s2[n] = picked(k)
            cp = pltpu.make_async_remote_copy(
                src_ref=s2.at[n], dst_ref=gat.at[l, zh, mine],
                send_sem=s2_send.at[n], recv_sem=s2_recv.at[zl, e],
                device_id=(peer, k), device_id_type=MESH)
            cp.start()
            sends.append(cp)

    def receive(dh):
        for source_zl, k in sources(dh):
            ref = gat.at[source_zl * NX + x, k // SIDE, pl.ds((k % SIDE) * TPD, TPD)]
            pltpu.make_async_remote_copy(
                src_ref=ref, dst_ref=ref, send_sem=s2_send.at[0], recv_sem=s2_recv.at[source_zl, k],
                device_id=across, device_id_type=MESH).wait_recv()

    pushed = [0]

    def part(src, q, half):
        if half is None:
            return gat.at[src, q]
        return gat.at[src, q, pl.ds(half * (BLK // 2), BLK // 2)]

    def push(src, q, to, half=None):
        ref = part(src, q, half)
        cp = pltpu.make_async_remote_copy(
            src_ref=ref, dst_ref=ref, send_sem=g_send.at[pushed[0]], recv_sem=g_recv.at[src, q, 0 if half is None else half],
            device_id=to, device_id_type=MESH)
        cp.start()
        pushed[0] += 1
        sends.append(cp)

    def arrive(src, q, half=None):
        ref = part(src, q, half)
        pltpu.make_async_remote_copy(
            src_ref=ref, dst_ref=ref, send_sem=g_send.at[0], recv_sem=g_recv.at[src, q, 0 if half is None else half],
            device_id=across, device_id_type=MESH).wait_recv()

    def add(src, q):
        def row(a, carry):
            at = pl.multiple_of((q * ROW_TILES + a) * LANE + src * SLAB, SLAB)
            for b in range(8):
                cols = pl.ds(b * LANE, LANE)
                out[pl.ds(at, SLAB), cols] = (
                    res[pl.ds(at, SLAB), cols].astype(jnp.float32) + gat[src, q, a * 8 + b].astype(jnp.float32)
                ).astype(jnp.bfloat16)
            return carry
        lax.fori_loop(0, ROW_TILES, row, 0)

    q1 = (zh + 3 + 2 * zl) % NH
    v1 = (zh + 1 + 2 * zl) % NH
    q2 = (zh + 2) % NH
    other = 1 - zl
    U = [(zl, zh), (zl, q1), (other, q1), (other, q2)]
    V = [(other, zh), (other, v1), (zl, v1), (zl, q2)]

    def at(unit, dx):
        return (unit[0] * NX + (x + dx) % NX, unit[1])

    def spread(unit):
        push(*at(unit, 0), right)
        push(*at(unit, 0), left)

    def relay(unit):
        arrive(*at(unit, 3))
        push(*at(unit, 3), right, 0)
        arrive(*at(unit, 1))
        push(*at(unit, 1), left, 1)

    def added(unit, *steps):
        for dx in steps:
            add(*at(unit, dx))

    def finish(unit):
        arrive(*at(unit, 2), 0)
        arrive(*at(unit, 2), 1)
        add(*at(unit, 2))

    send_to(0)
    gat[l, zh, mine] = picked(e)
    send_to(1)
    send_to(3)
    receive(0)
    spread(U[0])
    send_to(2)
    added(U[0], 0)
    relay(U[0])
    added(U[0], 3, 1)
    for n, dh in ((2, 3), (1, 1)):
        receive(dh)
        push(*at(U[n], 0), across)
        spread(U[n])
        added(U[n], 0)
    finish(U[0])
    for n in (2, 1):
        relay(U[n])
        added(U[n], 3, 1)
    receive(2)
    push(*at(U[3], 0), across)
    spread(U[3])
    added(U[3], 0)
    for dx in range(NX):
        push(*at(U[0], dx), across)
    for n in (2, 1):
        arrive(*at(V[n], 0))
        spread(V[n])
        added(V[n], 0)
    relay(U[3])
    added(U[3], 3, 1)
    finish(U[2])
    finish(U[1])
    arrive(*at(V[3], 0))
    spread(V[3])
    added(V[3], 0)
    for n in (2, 1):
        relay(V[n])
        added(V[n], 3, 1)
    finish(U[3])
    relay(V[3])
    added(V[3], 3, 1)
    for dx in range(NX):
        arrive(*at(V[0], dx))
        added(V[0], dx)
    for n in (2, 1, 3):
        finish(V[n])
    for cp in sends:
        cp.wait_send()


N_PUSH = 2 + 2 + 4 + 3 * (3 + 2 + 2 + 2)


def on_device(update, resident, placement, counts):
    _, rows, cols = resident.shape
    bf16 = jnp.bfloat16
    dma = pltpu.SemaphoreType.DMA
    result = pl.pallas_call(
        kernel,
        out_shape=pltpu.VMEM((rows, cols), bf16),
        in_specs=[pl.BlockSpec(memory_space=pltpu.HBM)] * 4,
        out_specs=pl.BlockSpec(memory_space=pltpu.VMEM),
        scratch_shapes=[
            pltpu.VMEM((EXP * TPD, LANE, LANE), jnp.float32),
            pltpu.VMEM((rows, cols), bf16),
            pltpu.VMEM((NL, EXP * TPD, SLAB, LANE), bf16),
            pltpu.VMEM((NL, EXP * TPD, SLAB, LANE), bf16),
            pltpu.VMEM((NE - 1, TPD, SLAB, LANE), bf16),
            pltpu.VMEM((NL, NH, BLK, SLAB, LANE), bf16),
            pltpu.SMEM((NE,), jnp.int32),
            pltpu.SMEM((NE,), jnp.int32),
            pltpu.SMEM((NE,), jnp.int32),
            dma((4,)),
            dma((NL - 1,)),
            dma((NL,)),
            dma((NE - 1,)),
            dma((NZ, NE)),
            dma((N_PUSH,)),
            dma((NL, NH, 2)),
        ],
        compiler_params=pltpu.CompilerParams(collective_id=0, has_side_effects=True, vmem_limit_bytes=VMEM_LIMIT),
        name="refresh",
    )(*(pltpu.with_memory_space_constraint(a, pltpu.HBM) for a in (update.reshape(EXP * TPD, LANE, LANE), resident.reshape(rows, cols), placement, counts)))
    return result[None]


def solution(mesh):
    placed = (P("learn", "expert", None, None), P("expert", None, None), P(), P())
    return jax.shard_map(
        on_device, mesh=mesh, in_specs=placed, out_specs=P("expert", None, None), check_vma=False
    )
```

```python
import jax
import jax.numpy as jnp
from jax import lax
from jax.experimental import pallas as pl
from jax.experimental.pallas import tpu as pltpu
from jax.sharding import PartitionSpec as P

MESH = pl.DeviceIdType.MESH
NX, NZ, NH, NY, NC = 4, 2, 4, 4, 2
NL, NE = 8, 32
EXP, PER, TPD = 4, 8, 5
SLAB, LANE = 16, 128
SIDE = NY * NC
VMEM_LIMIT = 48 << 20
PARTS = ((0, 3), (3, 2))
WHOLE = (0, TPD)
ROW_TILES = 5


def kernel(update, resident, placement_in, counts_in, out,
           upd, res, s1a, s1b, r1a, r1b, s2, gat, placement, counts, owner,
           in_sem, s1_send, s1_recv, s2_send, s2_recv, g_send, g_recv):
    l = lax.axis_index("learn")
    e = lax.axis_index("expert")
    zl, x = l // NX, l % NX
    zh, y, c = e // (NY * NC), (e // NC) % NY, e % NC
    right = (zl * NX + (x + 1) % NX, e)
    left = (zl * NX + (x + 3) % NX, e)
    across = ((1 - zl) * NX + x, e)

    ins = []
    for n, (src, dst) in enumerate(((counts_in, counts), (update, upd), (placement_in, placement), (resident, res))):
        cp = pltpu.make_async_copy(src, dst, in_sem.at[n])
        cp.start()
        ins.append(cp)
    counts_ready, upd_ready, placement_ready, res_ready = ins

    learn_peers = [(((zl + dz) % NZ) * NX + (x + dx) % NX) for dz in range(NZ) for dx in range(NX) if (dz, dx) != (0, 0)]

    def slot(dh, n):
        return ((zh + dh) % NH) * SIDE + (((y + n // NC) % NY) * NC + (c + n) % NC)

    def zl_at(dh):
        return {0: zl, 1: 0, 3: 1, 2: 1 - zl}[dh]

    def sources(dh):
        back = (4 - dh) % NH
        if dh == 0:
            return [(zl, slot(0, n)) for n in range(1, SIDE)]
        if dh == 2:
            return [(1 - zl, slot(2, n)) for n in range(SIDE)]
        at = (zh + 3 + 2 * zl) % NH
        source_zl = zl if dh == 1 else 1 - zl
        return [(source_zl, at * SIDE + slot(0, n) % SIDE) for n in range(SIDE)]

    targets = {dh: [(zl_at(dh) * NX + x, slot(dh, n)) for n in range(1 if dh == 0 else 0, SIDE)] for dh in (0, 1, 3, 2)}

    barrier = pltpu.get_barrier_semaphore()
    for peer in learn_peers:
        pl.semaphore_signal(barrier, inc=1, device_id=(peer, e), device_id_type=MESH)
    for dh in (0, 1, 3, 2):
        for source_zl, k in sources(dh):
            pl.semaphore_signal(barrier, inc=1, device_id=(source_zl * NX + x, k), device_id_type=MESH)

    s1, r1 = (s1a, s1b), (r1a, r1b)

    counts_ready.wait()
    upd_ready.wait()

    def encode_part(p):
        first, size = PARTS[p]

        def encode(n, carry):
            i, m = n // size, n % size
            j = first + m
            u = upd[i, j]
            largest = jnp.max(jnp.abs(u), axis=(0, 1), keepdims=True)
            scale = ((largest + 1e-06) / 448.0).astype(jnp.bfloat16).astype(jnp.float32)
            code = (u * (1.0 / scale)).astype(jnp.bfloat16).astype(jnp.float32)
            changed = jnp.where(e * TPD + j < counts[l * EXP + i], 1.0, 0.0).astype(jnp.float32)
            s1[p][:, i, m] = (code * (scale * changed)).astype(jnp.bfloat16).reshape(NL, SLAB, LANE)
            return carry

        lax.fori_loop(0, EXP * size, encode, 0, unroll=4)

    def wait_for(ref, sem):
        pltpu.make_async_copy(ref, ref, sem).wait()

    def exchange(p):
        for peer in learn_peers:
            cp = pltpu.make_async_remote_copy(
                src_ref=s1[p].at[peer], dst_ref=r1[p].at[l],
                send_sem=s1_send.at[p], recv_sem=s1_recv.at[p],
                device_id=(peer, e), device_id_type=MESH)
            cp.start()

    def exchanged(p):
        wait_for(r1[p].at[pl.ds(0, NL - 1)], s1_recv.at[p])

    encode_part(0)
    pl.semaphore_wait(barrier, NL - 1 + NE - 1)
    exchange(0)
    encode_part(1)
    exchange(1)
    for p in range(2):
        r1[p][l] = s1[p][l]
    placement_ready.wait()

    def owner_of(k, carry):
        def step(n, best):
            return jnp.maximum(best, jnp.where(placement[n] == k, n, 0))
        owner[k] = lax.fori_loop(0, NE, step, 0, unroll=True)
        return carry

    lax.fori_loop(0, NE, owner_of, 0)
    res_ready.wait()

    me = y * NC + c

    def pick(ref, k, span):
        o = owner[k]
        for p, part in enumerate(PARTS):
            if span in (part, WHOLE):
                ref[pl.ds(*part)] = r1[p][o // EXP, o % EXP]

    def send_to(dh, span, p):
        group = {0: 0, 1: jnp.where(zl == 0, 1, 2), 3: jnp.where(zl == 1, 1, 2), 2: 3}[dh]
        for m, (peer, k) in enumerate(targets[dh]):
            n = ORDER[dh] + m
            pick(s2.at[n], k, span)
            pltpu.make_async_remote_copy(
                src_ref=s2.at[n, pl.ds(*span)], dst_ref=gat.at[l, zh, me, pl.ds(*span)],
                send_sem=s2_send, recv_sem=s2_recv.at[p, group],
                device_id=(peer, k), device_id_type=MESH).start()

    def own_part(span):
        pick(gat.at[l, zh, me], e, span)

    def receive(group, span, p):
        first = 1 if group == 0 else 0
        wait_for(gat.at[l, zh, pl.ds(first, SIDE - first), pl.ds(*span)], s2_recv.at[p, group])

    def piece(src, q, span, half):
        if half is None:
            return gat.at[src, q, :, pl.ds(*span)]
        return gat.at[src, q, pl.ds(half * (SIDE // 2), SIDE // 2), pl.ds(*span)]

    def slot_of(span, half):
        return (1 if span == PARTS[1] else 0) * 2 + (half or 0)

    def push(src, q, span, to, half=None):
        ref = piece(src, q, span, half)
        pltpu.make_async_remote_copy(
            src_ref=ref, dst_ref=ref, send_sem=g_send, recv_sem=g_recv.at[src, q, slot_of(span, half)],
            device_id=to, device_id_type=MESH).start()

    def arrive(src, q, span, half=None):
        wait_for(piece(src, q, span, half), g_recv.at[src, q, slot_of(span, half)])

    def add(src, q):
        def row(a, carry):
            at = pl.multiple_of((q * ROW_TILES + a) * LANE + src * SLAB, SLAB)
            for b in range(8):
                cols = pl.ds(b * LANE, LANE)
                t = a * 8 + b
                out[pl.ds(at, SLAB), cols] = (
                    res[pl.ds(at, SLAB), cols].astype(jnp.float32) + gat[src, q, t // TPD, t % TPD].astype(jnp.float32)
                ).astype(jnp.bfloat16)
            return carry
        lax.fori_loop(0, ROW_TILES, row, 0)

    q1 = (zh + 3 + 2 * zl) % NH
    v1 = (zh + 1 + 2 * zl) % NH
    q2 = (zh + 2) % NH
    other = 1 - zl
    U = [(zl, zh), (zl, q1), (other, q1), (other, q2)]
    V = [(other, zh), (other, v1), (zl, v1), (zl, q2)]
    A, B = PARTS

    def at(unit, dx):
        return (unit[0] * NX + (x + dx) % NX, unit[1])

    def spread(unit, span):
        push(*at(unit, 0), span, right)
        push(*at(unit, 0), span, left)

    def relay(unit, *spans):
        for dx, to, half in ((3, right, 0), (1, left, 1)):
            for span in spans:
                arrive(*at(unit, dx), span)
            push(*at(unit, dx), WHOLE, to, half)

    def added(unit, *steps):
        for dx in steps:
            add(*at(unit, dx))

    def finish(unit):
        arrive(*at(unit, 2), WHOLE, 0)
        arrive(*at(unit, 2), WHOLE, 1)
        add(*at(unit, 2))

    def cross(unit):
        push(*at(unit, 0), WHOLE, across)

    def crossed(unit):
        arrive(*at(unit, 0), WHOLE)
        spread(unit, WHOLE)

    exchanged(0)
    send_to(0, A, 0)
    own_part(A)
    send_to(1, A, 0)
    send_to(3, A, 0)
    receive(0, A, 0)
    spread(U[0], A)
    exchanged(1)
    send_to(0, B, 1)
    own_part(B)
    send_to(1, B, 1)
    send_to(3, B, 1)
    receive(0, B, 1)
    spread(U[0], B)
    send_to(2, WHOLE, 0)
    added(U[0], 0)
    for n in (2, 1):
        receive(n, A, 0)
        spread(U[n], A)
    relay(U[0], A, B)
    added(U[0], 3, 1)
    for n in (2, 1):
        receive(n, B, 1)
        cross(U[n])
        spread(U[n], B)
        added(U[n], 0)
    finish(U[0])
    for n in (2, 1):
        relay(U[n], A, B)
        added(U[n], 3, 1)
    for n in (2, 1):
        crossed(V[n])
        added(V[n], 0)
    receive(3, WHOLE, 0)
    cross(U[3])
    spread(U[3], WHOLE)
    added(U[3], 0)
    for dx in range(NX):
        push(*at(U[0], dx), WHOLE, across)
    for n in (2, 1):
        finish(U[n])
        relay(V[n], WHOLE)
        added(V[n], 3, 1)
    relay(U[3], WHOLE)
    added(U[3], 3, 1)
    crossed(V[3])
    added(V[3], 0)
    for n in (2, 1):
        finish(V[n])
    finish(U[3])
    relay(V[3], WHOLE)
    added(V[3], 3, 1)
    for dx in range(NX):
        arrive(*at(V[0], dx), WHOLE)
        added(V[0], dx)
    for p in range(2):
        wait_for(s1[p].at[pl.ds(0, NL - 1)], s1_send.at[p])
    wait_for(s2, s2_send)
    finish(V[3])
    wait_for(gat.at[pl.ds(0, NL - 1)], g_send)


ORDER = {0: 0, 1: SIDE - 1, 3: 2 * SIDE - 1, 2: 3 * SIDE - 1}


def on_device(update, resident, placement, counts):
    _, rows, cols = resident.shape
    bf16 = jnp.bfloat16
    dma = pltpu.SemaphoreType.DMA
    result = pl.pallas_call(
        kernel,
        out_shape=pltpu.VMEM((rows, cols), bf16),
        in_specs=[pl.BlockSpec(memory_space=pltpu.HBM)] * 4,
        out_specs=pl.BlockSpec(memory_space=pltpu.VMEM),
        scratch_shapes=[
            pltpu.VMEM((EXP, TPD, LANE, LANE), jnp.float32),
            pltpu.VMEM((rows, cols), bf16),
            *[pltpu.VMEM((NL, EXP, size, SLAB, LANE), bf16) for _ in range(2) for _, size in PARTS],
            pltpu.VMEM((NE - 1, TPD, SLAB, LANE), bf16),
            pltpu.VMEM((NL, NH, SIDE, TPD, SLAB, LANE), bf16),
            pltpu.SMEM((NE,), jnp.int32),
            pltpu.SMEM((NE,), jnp.int32),
            pltpu.SMEM((NE,), jnp.int32),
            dma((4,)),
            dma((2,)),
            dma((2,)),
            dma,
            dma((2, 4)),
            dma,
            dma((NL, NH, 4)),
        ],
        compiler_params=pltpu.CompilerParams(collective_id=0, has_side_effects=True, vmem_limit_bytes=VMEM_LIMIT),
        name="refresh",
    )(*(pltpu.with_memory_space_constraint(a, pltpu.HBM) for a in (update, resident.reshape(rows, cols), placement, counts)))
    return result[None]


def solution(mesh):
    placed = (P("learn", "expert", None, None), P("expert", None, None), P(), P())
    return jax.shard_map(
        on_device, mesh=mesh, in_specs=placed, out_specs=P("expert", None, None), check_vma=False
    )
```

```python
import jax
import jax.numpy as jnp
from jax import lax
from jax.experimental import pallas as pl
from jax.experimental.pallas import tpu as pltpu
from jax.sharding import PartitionSpec as P

MESH = pl.DeviceIdType.MESH
NX, NZ, NH, NY, NC = 4, 2, 4, 4, 2
NL, NE = 8, 32
EXP, PER, TPD = 4, 8, 5
SLAB, LANE = 16, 128
SIDE = NY * NC
VMEM_LIMIT = 48 << 20
PARTS = ((0, 2), (2, 3))
WHOLE = (0, TPD)
ROW_TILES = 5


def kernel(update, resident, placement_in, counts_in, out,
           upd, res, s1a, s1b, r1a, r1b, s2, gat, placement, counts, owner,
           in_sem, s1_send, s1_recv, s2_send, s2_recv, g_send, g_recv):
    l = lax.axis_index("learn")
    e = lax.axis_index("expert")
    zl, x = l // NX, l % NX
    zh, y, c = e // (NY * NC), (e // NC) % NY, e % NC
    right = (zl * NX + (x + 1) % NX, e)
    left = (zl * NX + (x + 3) % NX, e)
    across = ((1 - zl) * NX + x, e)

    ins = []
    for n, (src, dst) in enumerate(((counts_in, counts), (update, upd), (placement_in, placement), (resident, res))):
        cp = pltpu.make_async_copy(src, dst, in_sem.at[n])
        cp.start()
        ins.append(cp)
    counts_ready, upd_ready, placement_ready, res_ready = ins

    learn_peers = [(((zl + dz) % NZ) * NX + (x + dx) % NX) for dz in range(NZ) for dx in range(NX) if (dz, dx) != (0, 0)]

    def slot(dh, n):
        return ((zh + dh) % NH) * SIDE + (((y + n // NC) % NY) * NC + (c + n) % NC)

    def zl_at(dh):
        return {0: zl, 1: 0, 3: 1, 2: 1 - zl}[dh]

    def sources(dh):
        back = (4 - dh) % NH
        if dh == 0:
            return [(zl, slot(0, n)) for n in range(1, SIDE)]
        if dh == 2:
            return [(1 - zl, slot(2, n)) for n in range(SIDE)]
        at = (zh + 3 + 2 * zl) % NH
        source_zl = zl if dh == 1 else 1 - zl
        return [(source_zl, at * SIDE + slot(0, n) % SIDE) for n in range(SIDE)]

    targets = {dh: [(zl_at(dh) * NX + x, slot(dh, n)) for n in range(1 if dh == 0 else 0, SIDE)] for dh in (0, 1, 3, 2)}

    barrier = pltpu.get_barrier_semaphore()
    for peer in learn_peers:
        pl.semaphore_signal(barrier, inc=1, device_id=(peer, e), device_id_type=MESH)
    for dh in (0, 1, 3, 2):
        for source_zl, k in sources(dh):
            pl.semaphore_signal(barrier, inc=1, device_id=(source_zl * NX + x, k), device_id_type=MESH)

    s1, r1 = (s1a, s1b), (r1a, r1b)

    counts_ready.wait()
    upd_ready.wait()

    def encode_part(p):
        first, size = PARTS[p]

        def encode(n, carry):
            i, m = n // size, n % size
            j = first + m
            u = upd[i, j]
            largest = jnp.max(jnp.abs(u), axis=(0, 1), keepdims=True)
            scale = ((largest + 1e-06) / 448.0).astype(jnp.bfloat16).astype(jnp.float32)
            code = (u * (1.0 / scale)).astype(jnp.bfloat16).astype(jnp.float32)
            changed = jnp.where(e * TPD + j < counts[l * EXP + i], 1.0, 0.0).astype(jnp.float32)
            s1[p][:, i, m] = (code * (scale * changed)).astype(jnp.bfloat16).reshape(NL, SLAB, LANE)
            return carry

        lax.fori_loop(0, EXP * size, encode, 0, unroll=4)

    def wait_for(ref, sem):
        pltpu.make_async_copy(ref, ref, sem).wait()

    def exchange(p):
        for peer in learn_peers:
            cp = pltpu.make_async_remote_copy(
                src_ref=s1[p].at[peer], dst_ref=r1[p].at[l],
                send_sem=s1_send.at[p], recv_sem=s1_recv.at[p],
                device_id=(peer, e), device_id_type=MESH)
            cp.start()

    def exchanged(p):
        wait_for(r1[p].at[pl.ds(0, NL - 1)], s1_recv.at[p])

    encode_part(0)
    pl.semaphore_wait(barrier, NL - 1 + NE - 1)
    exchange(0)
    encode_part(1)
    exchange(1)
    for p in range(2):
        r1[p][l] = s1[p][l]
    placement_ready.wait()

    def owner_of(k, carry):
        def step(n, best):
            return jnp.maximum(best, jnp.where(placement[n] == k, n, 0))
        owner[k] = lax.fori_loop(0, NE, step, 0, unroll=True)
        return carry

    lax.fori_loop(0, NE, owner_of, 0)
    res_ready.wait()

    me = y * NC + c

    def pick(ref, k, span):
        o = owner[k]
        for p, part in enumerate(PARTS):
            if span in (part, WHOLE):
                ref[pl.ds(*part)] = r1[p][o // EXP, o % EXP]

    def send_to(dh, span, p):
        group = {0: 0, 1: jnp.where(zl == 0, 1, 2), 3: jnp.where(zl == 1, 1, 2), 2: 3}[dh]
        for m, (peer, k) in enumerate(targets[dh]):
            n = ORDER[dh] + m
            pick(s2.at[n], k, span)
            pltpu.make_async_remote_copy(
                src_ref=s2.at[n, pl.ds(*span)], dst_ref=gat.at[l, zh, me, pl.ds(*span)],
                send_sem=s2_send, recv_sem=s2_recv.at[p, group],
                device_id=(peer, k), device_id_type=MESH).start()

    def own_part(span):
        pick(gat.at[l, zh, me], e, span)

    def receive(group, span, p):
        first = 1 if group == 0 else 0
        wait_for(gat.at[l, zh, pl.ds(first, SIDE - first), pl.ds(*span)], s2_recv.at[p, group])

    def piece(src, q, span, half):
        if half is None:
            return gat.at[src, q, :, pl.ds(*span)]
        return gat.at[src, q, pl.ds(half * (SIDE // 2), SIDE // 2), pl.ds(*span)]

    def slot_of(span, half):
        return (1 if span == PARTS[1] else 0) * 2 + (half or 0)

    def push(src, q, span, to, half=None):
        ref = piece(src, q, span, half)
        pltpu.make_async_remote_copy(
            src_ref=ref, dst_ref=ref, send_sem=g_send, recv_sem=g_recv.at[src, q, slot_of(span, half)],
            device_id=to, device_id_type=MESH).start()

    def arrive(src, q, span, half=None):
        wait_for(piece(src, q, span, half), g_recv.at[src, q, slot_of(span, half)])

    def add(src, q):
        def row(a, carry):
            at = pl.multiple_of((q * ROW_TILES + a) * LANE + src * SLAB, SLAB)
            for b in range(8):
                cols = pl.ds(b * LANE, LANE)
                t = a * 8 + b
                out[pl.ds(at, SLAB), cols] = (
                    res[pl.ds(at, SLAB), cols].astype(jnp.float32) + gat[src, q, t // TPD, t % TPD].astype(jnp.float32)
                ).astype(jnp.bfloat16)
            return carry
        lax.fori_loop(0, ROW_TILES, row, 0)

    q1 = (zh + 3 + 2 * zl) % NH
    v1 = (zh + 1 + 2 * zl) % NH
    q2 = (zh + 2) % NH
    other = 1 - zl
    U = [(zl, zh), (zl, q1), (other, q1), (other, q2)]
    V = [(other, zh), (other, v1), (zl, v1), (zl, q2)]
    A, B = PARTS

    def at(unit, dx):
        return (unit[0] * NX + (x + dx) % NX, unit[1])

    def spread(unit, span):
        push(*at(unit, 0), span, right)
        push(*at(unit, 0), span, left)

    def relay(unit, span):
        for dx, to, half in ((3, right, 0), (1, left, 1)):
            arrive(*at(unit, dx), span)
            push(*at(unit, dx), span, to, half)

    def added(unit, *steps):
        for dx in steps:
            add(*at(unit, dx))

    def finish(unit, *spans):
        for span in spans:
            for half in range(2):
                arrive(*at(unit, 2), span, half)
        add(*at(unit, 2))

    def cross(unit, dx=0):
        push(*at(unit, dx), WHOLE, across)

    def crossed(unit):
        arrive(*at(unit, 0), WHOLE)
        spread(unit, WHOLE)

    def take(unit, *steps):
        for dx in steps:
            arrive(*at(unit, dx), WHOLE)
            add(*at(unit, dx))

    exchanged(0)
    send_to(0, A, 0)
    own_part(A)
    exchanged(1)
    send_to(0, B, 1)
    own_part(B)
    send_to(1, A, 0)
    send_to(3, A, 0)
    receive(0, A, 0)
    spread(U[0], A)
    send_to(1, B, 1)
    send_to(3, B, 1)
    receive(0, B, 1)
    spread(U[0], B)
    cross(U[0])
    send_to(2, WHOLE, 0)
    added(U[0], 0)
    relay(U[0], A)
    for n in (2, 1):
        receive(n, A, 0)
        spread(U[n], A)
    relay(U[0], B)
    added(U[0], 3, 1)
    for n in (2, 1):
        receive(n, B, 1)
        cross(U[n])
        spread(U[n], B)
        added(U[n], 0)
    for n in (2, 1):
        relay(U[n], A)
    finish(U[0], A, B)
    for n in (2, 1):
        relay(U[n], B)
        added(U[n], 3, 1)
    for n in (2, 1):
        crossed(V[n])
        added(V[n], 0)
    receive(3, WHOLE, 0)
    cross(U[3])
    spread(U[3], WHOLE)
    added(U[3], 0)
    cross(U[0], 1)
    finish(U[2], A, B)
    cross(U[2], 2)
    cross(U[0], 3)
    cross(U[0], 2)
    finish(U[1], A, B)
    take(V[2], 3, 1)
    relay(V[1], WHOLE)
    added(V[1], 3, 1)
    crossed(V[3])
    added(V[3], 0)
    relay(U[3], WHOLE)
    added(U[3], 3, 1)
    take(V[2], 2)
    finish(V[1], WHOLE)
    take(V[0], 0, 1)
    relay(V[3], WHOLE)
    added(V[3], 3, 1)
    finish(U[3], WHOLE)
    take(V[0], 3, 2)
    finish(V[3], WHOLE)
    for p in range(2):
        wait_for(s1[p].at[pl.ds(0, NL - 1)], s1_send.at[p])
    wait_for(s2, s2_send)
    wait_for(gat.at[pl.ds(0, NL - 1)], g_send)


ORDER = {0: 0, 1: SIDE - 1, 3: 2 * SIDE - 1, 2: 3 * SIDE - 1}


def on_device(update, resident, placement, counts):
    _, rows, cols = resident.shape
    bf16 = jnp.bfloat16
    dma = pltpu.SemaphoreType.DMA
    result = pl.pallas_call(
        kernel,
        out_shape=pltpu.VMEM((rows, cols), bf16),
        in_specs=[pl.BlockSpec(memory_space=pltpu.HBM)] * 4,
        out_specs=pl.BlockSpec(memory_space=pltpu.VMEM),
        scratch_shapes=[
            pltpu.VMEM((EXP, TPD, LANE, LANE), jnp.float32),
            pltpu.VMEM((rows, cols), bf16),
            *[pltpu.VMEM((NL, EXP, size, SLAB, LANE), bf16) for _ in range(2) for _, size in PARTS],
            pltpu.VMEM((NE - 1, TPD, SLAB, LANE), bf16),
            pltpu.VMEM((NL, NH, SIDE, TPD, SLAB, LANE), bf16),
            pltpu.SMEM((NE,), jnp.int32),
            pltpu.SMEM((NE,), jnp.int32),
            pltpu.SMEM((NE,), jnp.int32),
            dma((4,)),
            dma((2,)),
            dma((2,)),
            dma,
            dma((2, 4)),
            dma,
            dma((NL, NH, 4)),
        ],
        compiler_params=pltpu.CompilerParams(collective_id=0, has_side_effects=True, vmem_limit_bytes=VMEM_LIMIT),
        name="refresh",
    )(*(pltpu.with_memory_space_constraint(a, pltpu.HBM) for a in (update, resident.reshape(rows, cols), placement, counts)))
    return result[None]


def solution(mesh):
    placed = (P("learn", "expert", None, None), P("expert", None, None), P(), P())
    return jax.shard_map(
        on_device, mesh=mesh, in_specs=placed, out_specs=P("expert", None, None), check_vma=False
    )
```

```python
import jax
import jax.numpy as jnp
from jax import lax
from jax.experimental import pallas as pl
from jax.experimental.pallas import tpu as pltpu
from jax.sharding import PartitionSpec as P

MESH = pl.DeviceIdType.MESH
NX, NZ, NH, NY, NC = 4, 2, 4, 4, 2
NL, NE = 8, 32
EXP, PER, TPD = 4, 8, 5
SLAB, LANE = 16, 128
SIDE = NY * NC
VMEM_LIMIT = 48 << 20
PARTS = ((0, 2), (2, 3))
WHOLE = (0, TPD)
ROW_TILES = 5


def kernel(update, resident, placement_in, counts_in, out,
           upd, res, s1a, s1b, r1a, r1b, s2, gat, placement, counts, inverse, owner,
           in_sem, s1_send, s1_recv, s2_send, s2_recv, g_send, g_recv):
    l = lax.axis_index("learn")
    e = lax.axis_index("expert")
    zl, x = l // NX, l % NX
    zh, y, c = e // (NY * NC), (e // NC) % NY, e % NC
    right = (zl * NX + (x + 1) % NX, e)
    left = (zl * NX + (x + 3) % NX, e)
    across = ((1 - zl) * NX + x, e)

    ins = []
    for n, (src, dst) in enumerate(((counts_in, counts), (update, upd), (placement_in, placement), (resident, res))):
        cp = pltpu.make_async_copy(src, dst, in_sem.at[n])
        cp.start()
        ins.append(cp)
    counts_ready, upd_ready, placement_ready, res_ready = ins

    learn_peers = [(((zl + dz) % NZ) * NX + (x + dx) % NX) for dz in range(NZ) for dx in range(NX) if (dz, dx) != (0, 0)]

    def slot(dh, n):
        return ((zh + dh) % NH) * SIDE + (((y + n // NC) % NY) * NC + (c + n) % NC)

    step = 2 * zl - 1
    members = {0: (4, 5, 2, 3, 6, 7, 1)}
    for group in (1, 2, 3):
        members[group] = tuple(range(SIDE))

    def peers(group, forward):
        other = 1 - zl
        dh, to_zl = {0: (0, zl), 1: (NH - step if forward else NH + step, zl),
                     2: (NH + step, other), 3: (2, other)}[group]
        return [(to_zl * NX + x, slot(dh, n)) for n in members[group]]

    barrier = pltpu.get_barrier_semaphore()
    for peer in learn_peers:
        pl.semaphore_signal(barrier, inc=1, device_id=(peer, e), device_id_type=MESH)
    for group in (0, 2, 1, 3):
        for peer, k in peers(group, False):
            pl.semaphore_signal(barrier, inc=1, device_id=(peer, k), device_id_type=MESH)

    s1, r1 = (s1a, s1b), (r1a, r1b)

    counts_ready.wait()
    upd_ready.wait()

    def encode_part(p):
        first, size = PARTS[p]

        def encode(n, carry):
            i, m = n // size, n % size
            j = first + m
            u = upd[i, j]
            largest = jnp.max(jnp.abs(u), axis=(0, 1), keepdims=True)
            scale = ((largest + 1e-06) / 448.0).astype(jnp.bfloat16).astype(jnp.float32)
            code = (u * (1.0 / scale)).astype(jnp.bfloat16).astype(jnp.float32)
            changed = jnp.where(e * TPD + j < counts[l * EXP + i], 1.0, 0.0).astype(jnp.float32)
            s1[p][:, i, m] = (code * (scale * changed)).astype(jnp.bfloat16).reshape(NL, SLAB, LANE)
            return carry

        lax.fori_loop(0, EXP * size, encode, 0, unroll=4)

    def wait_for(ref, sem):
        pltpu.make_async_copy(ref, ref, sem).wait()

    def exchange(p):
        for peer in learn_peers:
            cp = pltpu.make_async_remote_copy(
                src_ref=s1[p].at[peer], dst_ref=r1[p].at[l],
                send_sem=s1_send.at[p], recv_sem=s1_recv.at[p],
                device_id=(peer, e), device_id_type=MESH)
            cp.start()

    def exchanged(p):
        wait_for(r1[p].at[pl.ds(0, NL - 1)], s1_recv.at[p])

    encode_part(0)
    pl.semaphore_wait(barrier, NL - 1 + NE - 1)
    exchange(0)
    encode_part(1)
    exchange(1)
    for p in range(2):
        r1[p][l] = s1[p][l]
    placement_ready.wait()
    ids = lax.broadcasted_iota(jnp.int32, (NE, NE), 1)
    slots = lax.broadcasted_iota(jnp.int32, (NE, NE), 0)
    held = jnp.where(placement[...] == slots, ids, 0)
    inverse[...] = jnp.broadcast_to(jnp.max(held, axis=1, keepdims=True), (NE, LANE))
    owner_in = pltpu.make_async_copy(inverse, owner, in_sem.at[4])
    owner_in.start()
    res_ready.wait()
    owner_in.wait()

    me = y * NC + c

    def pick(ref, k, span):
        o = owner[k, 0]
        for p, part in enumerate(PARTS):
            if span in (part, WHOLE):
                ref[pl.ds(*part)] = r1[p][o // EXP, o % EXP]

    def send_to(group, span, p):
        for m, (peer, k) in enumerate(peers(group, True)):
            n = FIRST[group] + m
            pick(s2.at[n], k, span)
            pltpu.make_async_remote_copy(
                src_ref=s2.at[n, pl.ds(*span)], dst_ref=gat.at[l, zh, me, pl.ds(*span)],
                send_sem=s2_send, recv_sem=s2_recv.at[p, group],
                device_id=(peer, k), device_id_type=MESH).start()

    def own_part(span):
        pick(gat.at[l, zh, me], e, span)

    def receive(group, span, p):
        first = 1 if group == 0 else 0
        wait_for(gat.at[l, zh, pl.ds(first, SIDE - first), pl.ds(*span)], s2_recv.at[p, group])

    def piece(src, q, span, half):
        if half is None:
            return gat.at[src, q, :, pl.ds(*span)]
        return gat.at[src, q, pl.ds(half * (SIDE // 2), SIDE // 2), pl.ds(*span)]

    def slot_of(span, half):
        return (1 if span == PARTS[1] else 0) * 2 + (half or 0)

    def push(src, q, span, to, half=None):
        ref = piece(src, q, span, half)
        pltpu.make_async_remote_copy(
            src_ref=ref, dst_ref=ref, send_sem=g_send, recv_sem=g_recv.at[src, q, slot_of(span, half)],
            device_id=to, device_id_type=MESH).start()

    def arrive(src, q, span, half=None):
        wait_for(piece(src, q, span, half), g_recv.at[src, q, slot_of(span, half)])

    def add(src, q):
        def row(a, carry):
            at = pl.multiple_of((q * ROW_TILES + a) * LANE + src * SLAB, SLAB)
            for b in range(8):
                cols = pl.ds(b * LANE, LANE)
                t = a * 8 + b
                out[pl.ds(at, SLAB), cols] = (
                    res[pl.ds(at, SLAB), cols].astype(jnp.float32) + gat[src, q, t // TPD, t % TPD].astype(jnp.float32)
                ).astype(jnp.bfloat16)
            return carry
        lax.fori_loop(0, ROW_TILES, row, 0)

    q1 = (zh + 3 + 2 * zl) % NH
    v1 = (zh + 1 + 2 * zl) % NH
    q2 = (zh + 2) % NH
    other = 1 - zl
    U = [(zl, zh), (zl, q1), (other, q1), (other, q2)]
    V = [(other, zh), (other, v1), (zl, v1), (zl, q2)]
    A, B = PARTS

    def at(unit, dx):
        return (unit[0] * NX + (x + dx) % NX, unit[1])

    def spread(unit, span):
        push(*at(unit, 0), span, right)
        push(*at(unit, 0), span, left)

    def relay(unit, span):
        for dx, to, half in ((3, right, 0), (1, left, 1)):
            arrive(*at(unit, dx), span)
            push(*at(unit, dx), span, to, half)

    def added(unit, *steps):
        for dx in steps:
            add(*at(unit, dx))

    def finish(unit, *spans):
        for span in spans:
            for half in range(2):
                arrive(*at(unit, 2), span, half)
        add(*at(unit, 2))

    def cross(unit, dx=0, span=WHOLE):
        push(*at(unit, dx), span, across)

    def crossed(unit, span=WHOLE):
        arrive(*at(unit, 0), span)
        spread(unit, span)

    def take(unit, *steps):
        for dx in steps:
            arrive(*at(unit, dx), WHOLE)
            add(*at(unit, dx))

    exchanged(0)
    send_to(0, A, 0)
    own_part(A)
    exchanged(1)
    send_to(0, B, 1)
    own_part(B)
    send_to(1, A, 0)
    send_to(2, A, 0)
    receive(0, A, 0)
    spread(U[0], A)
    send_to(1, B, 1)
    send_to(2, B, 1)
    receive(0, B, 1)
    spread(U[0], B)
    cross(U[0])
    send_to(3, A, 0)
    send_to(3, B, 1)
    added(U[0], 0)
    relay(U[0], A)
    for n in (1, 2):
        receive(n, A, 0)
        cross(U[n], 0, A)
        spread(U[n], A)
    relay(U[0], B)
    added(U[0], 3, 1)
    for n in (1, 2):
        receive(n, B, 1)
        cross(U[n], 0, B)
        spread(U[n], B)
        added(U[n], 0)
    for n in (2, 1):
        relay(U[n], A)
    for n in (2, 1):
        crossed(V[n], A)
    finish(U[0], A, B)
    for n in (2, 1):
        relay(U[n], B)
        added(U[n], 3, 1)
    receive(3, A, 0)
    cross(U[3], 0, A)
    spread(U[3], A)
    for n in (2, 1):
        crossed(V[n], B)
        added(V[n], 0)
    receive(3, B, 1)
    cross(U[3], 0, B)
    spread(U[3], B)
    added(U[3], 0)
    cross(U[0], 1)
    cross(U[0], 3)
    finish(U[2], A, B)
    cross(U[2], 2)
    cross(U[0], 2)
    finish(U[1], A, B)
    crossed(V[3], A)
    for n in (3, 1):
        for span in PARTS:
            arrive(*at(V[2], n), span)
        add(*at(V[2], n))
    relay(V[1], A)
    relay(V[1], B)
    added(V[1], 3, 1)
    crossed(V[3], B)
    added(V[3], 0)
    relay(U[3], A)
    relay(V[3], A)
    relay(U[3], B)
    added(U[3], 3, 1)
    relay(V[3], B)
    added(V[3], 3, 1)
    take(V[2], 2)
    finish(V[1], A, B)
    take(V[0], 0, 1)
    finish(U[3], A, B)
    take(V[0], 3, 2)
    finish(V[3], A, B)
    for p in range(2):
        wait_for(s1[p].at[pl.ds(0, NL - 1)], s1_send.at[p])
    wait_for(s2, s2_send)
    wait_for(gat.at[pl.ds(0, NL - 1)], g_send)


FIRST = {0: 0, 2: SIDE - 1, 1: 2 * SIDE - 1, 3: 3 * SIDE - 1}


def on_device(update, resident, placement, counts):
    _, rows, cols = resident.shape
    bf16 = jnp.bfloat16
    dma = pltpu.SemaphoreType.DMA
    result = pl.pallas_call(
        kernel,
        out_shape=pltpu.VMEM((rows, cols), bf16),
        in_specs=[pl.BlockSpec(memory_space=pltpu.HBM)] * 4,
        out_specs=pl.BlockSpec(memory_space=pltpu.VMEM),
        scratch_shapes=[
            pltpu.VMEM((EXP, TPD, LANE, LANE), jnp.float32),
            pltpu.VMEM((rows, cols), bf16),
            *[pltpu.VMEM((NL, EXP, size, SLAB, LANE), bf16) for _ in range(2) for _, size in PARTS],
            pltpu.VMEM((NE - 1, TPD, SLAB, LANE), bf16),
            pltpu.VMEM((NL, NH, SIDE, TPD, SLAB, LANE), bf16),
            pltpu.VMEM((1, NE), jnp.int32),
            pltpu.SMEM((NE,), jnp.int32),
            pltpu.VMEM((NE, LANE), jnp.int32),
            pltpu.SMEM((NE, LANE), jnp.int32),
            dma((5,)),
            dma((2,)),
            dma((2,)),
            dma,
            dma((2, 4)),
            dma,
            dma((NL, NH, 4)),
        ],
        compiler_params=pltpu.CompilerParams(collective_id=0, has_side_effects=True, vmem_limit_bytes=VMEM_LIMIT),
        name="refresh",
    )(*(pltpu.with_memory_space_constraint(a, pltpu.HBM) for a in (update, resident.reshape(rows, cols), placement.reshape(1, NE), counts)))
    return result[None]


def solution(mesh):
    placed = (P("learn", "expert", None, None), P("expert", None, None), P(), P())
    return jax.shard_map(
        on_device, mesh=mesh, in_specs=placed, out_specs=P("expert", None, None), check_vma=False
    )
```

```python
import jax
import jax.numpy as jnp
from jax import lax
from jax.experimental import pallas as pl
from jax.experimental.pallas import tpu as pltpu
from jax.sharding import PartitionSpec as P

MESH = pl.DeviceIdType.MESH
NX, NZ, NH, NY, NC = 4, 2, 4, 4, 2
NL, NE = 8, 32
EXP, PER, TPD = 4, 8, 5
SLAB, LANE = 16, 128
SIDE = NY * NC
VMEM_LIMIT = 48 << 20
PARTS = ((0, 2), (2, 3))
WHOLE = (0, TPD)
ROW_TILES = 5


def kernel(update, resident, placement_in, counts_in, out,
           upd, res, s1a, s1b, r1a, r1b, s2, gat, placement, counts, inverse, owner,
           in_sem, s1_send, s1_recv, s2_send, s2_recv, g_send, g_recv):
    l = lax.axis_index("learn")
    e = lax.axis_index("expert")
    zl, x = l // NX, l % NX
    zh, y, c = e // (NY * NC), (e // NC) % NY, e % NC
    right = (zl * NX + (x + 1) % NX, e)
    left = (zl * NX + (x + 3) % NX, e)
    across = ((1 - zl) * NX + x, e)

    ins = []
    for n, (src, dst) in enumerate(((counts_in, counts), (update, upd), (placement_in, placement), (resident, res))):
        cp = pltpu.make_async_copy(src, dst, in_sem.at[n])
        cp.start()
        ins.append(cp)
    counts_ready, upd_ready, placement_ready, res_ready = ins

    learn_peers = [(((zl + dz) % NZ) * NX + (x + dx) % NX) for dz in range(NZ) for dx in range(NX) if (dz, dx) != (0, 0)]

    def slot(dh, n):
        return ((zh + dh) % NH) * SIDE + (((y + n // NC) % NY) * NC + (c + n) % NC)

    step = 2 * zl - 1
    members = {0: (4, 5, 2, 3, 6, 7, 1)}
    for group in (1, 2, 3):
        members[group] = tuple(range(SIDE))

    def peers(group, forward):
        other = 1 - zl
        dh, to_zl = {0: (0, zl), 1: (NH - step if forward else NH + step, zl),
                     2: (NH + step, other), 3: (2, other)}[group]
        return [(to_zl * NX + x, slot(dh, n)) for n in members[group]]

    barrier = pltpu.get_barrier_semaphore()
    for peer in learn_peers:
        pl.semaphore_signal(barrier, inc=1, device_id=(peer, e), device_id_type=MESH)
    for group in (0, 2, 1, 3):
        for peer, k in peers(group, False):
            pl.semaphore_signal(barrier, inc=1, device_id=(peer, k), device_id_type=MESH)

    s1, r1 = (s1a, s1b), (r1a, r1b)

    counts_ready.wait()
    upd_ready.wait()

    def encode_part(p):
        first, size = PARTS[p]

        def encode(n, carry):
            i, m = n // size, n % size
            j = first + m
            u = upd[i, j]
            largest = jnp.max(jnp.abs(u), axis=(0, 1), keepdims=True)
            scale = ((largest + 1e-06) / 448.0).astype(jnp.bfloat16).astype(jnp.float32)
            code = (u * (1.0 / scale)).astype(jnp.bfloat16).astype(jnp.float32)
            changed = jnp.where(e * TPD + j < counts[l * EXP + i], 1.0, 0.0).astype(jnp.float32)
            s1[p][:, i, m] = (code * (scale * changed)).astype(jnp.bfloat16).reshape(NL, SLAB, LANE)
            return carry

        lax.fori_loop(0, EXP * size, encode, 0, unroll=4)

    def wait_for(ref, sem):
        pltpu.make_async_copy(ref, ref, sem).wait()

    def exchange(p):
        for peer in learn_peers:
            cp = pltpu.make_async_remote_copy(
                src_ref=s1[p].at[peer], dst_ref=r1[p].at[l],
                send_sem=s1_send.at[p], recv_sem=s1_recv.at[p],
                device_id=(peer, e), device_id_type=MESH)
            cp.start()

    def exchanged(p):
        wait_for(r1[p].at[pl.ds(0, NL - 1)], s1_recv.at[p])

    encode_part(0)
    pl.semaphore_wait(barrier, NL - 1 + NE - 1)
    exchange(0)
    encode_part(1)
    exchange(1)
    for p in range(2):
        r1[p][l] = s1[p][l]
    placement_ready.wait()
    ids = lax.broadcasted_iota(jnp.int32, (NE, NE), 1)
    slots = lax.broadcasted_iota(jnp.int32, (NE, NE), 0)
    held = jnp.where(placement[...] == slots, ids, 0)
    inverse[...] = jnp.broadcast_to(jnp.max(held, axis=1, keepdims=True), (NE, LANE))
    owner_in = pltpu.make_async_copy(inverse, owner, in_sem.at[4])
    owner_in.start()
    res_ready.wait()
    owner_in.wait()

    me = y * NC + c

    def pick(ref, k, span):
        o = owner[k, 0]
        for p, part in enumerate(PARTS):
            if span in (part, WHOLE):
                ref[pl.ds(*part)] = r1[p][o // EXP, o % EXP]

    def send_to(group, span, p):
        for m, (peer, k) in enumerate(peers(group, True)):
            n = FIRST[group] + m
            pick(s2.at[n], k, span)
            pltpu.make_async_remote_copy(
                src_ref=s2.at[n, pl.ds(*span)], dst_ref=gat.at[l, zh, me, pl.ds(*span)],
                send_sem=s2_send, recv_sem=s2_recv.at[p, group],
                device_id=(peer, k), device_id_type=MESH).start()

    def own_part(span):
        pick(gat.at[l, zh, me], e, span)

    def receive(group, span, p):
        first = 1 if group == 0 else 0
        wait_for(gat.at[l, zh, pl.ds(first, SIDE - first), pl.ds(*span)], s2_recv.at[p, group])

    def piece(src, q, span, half):
        if half is None:
            return gat.at[src, q, :, pl.ds(*span)]
        return gat.at[src, q, pl.ds(half * (SIDE // 2), SIDE // 2), pl.ds(*span)]

    def slot_of(span, half):
        return (1 if span == PARTS[1] else 0) * 2 + (half or 0)

    def push(src, q, span, to, half=None):
        ref = piece(src, q, span, half)
        pltpu.make_async_remote_copy(
            src_ref=ref, dst_ref=ref, send_sem=g_send, recv_sem=g_recv.at[src, q, slot_of(span, half)],
            device_id=to, device_id_type=MESH).start()

    def arrive(src, q, span, half=None):
        wait_for(piece(src, q, span, half), g_recv.at[src, q, slot_of(span, half)])

    def add(src, q):
        def row(a, carry):
            at = pl.multiple_of((q * ROW_TILES + a) * LANE + src * SLAB, SLAB)
            for b in range(8):
                cols = pl.ds(b * LANE, LANE)
                t = a * 8 + b
                out[pl.ds(at, SLAB), cols] = (
                    res[pl.ds(at, SLAB), cols].astype(jnp.float32) + gat[src, q, t // TPD, t % TPD].astype(jnp.float32)
                ).astype(jnp.bfloat16)
            return carry
        lax.fori_loop(0, ROW_TILES, row, 0)

    q1 = (zh + 3 + 2 * zl) % NH
    v1 = (zh + 1 + 2 * zl) % NH
    q2 = (zh + 2) % NH
    other = 1 - zl
    U = [(zl, zh), (zl, q1), (other, q1), (other, q2)]
    V = [(other, zh), (other, v1), (zl, v1), (zl, q2)]
    A, B = PARTS

    def at(unit, dx):
        return (unit[0] * NX + (x + dx) % NX, unit[1])

    def spread(unit, span):
        push(*at(unit, 0), span, right)
        push(*at(unit, 0), span, left)

    def relay(unit, span):
        for dx, to, half in ((3, right, 0), (1, left, 1)):
            arrive(*at(unit, dx), span)
            push(*at(unit, dx), span, to, half)

    def added(unit, *steps):
        for dx in steps:
            add(*at(unit, dx))

    def finish(unit, *spans):
        for span in spans:
            for half in range(2):
                arrive(*at(unit, 2), span, half)
        add(*at(unit, 2))

    def cross(unit, dx=0, span=WHOLE):
        push(*at(unit, dx), span, across)

    def crossed(unit, span=WHOLE):
        arrive(*at(unit, 0), span)
        spread(unit, span)

    def take(unit, *steps):
        for dx in steps:
            arrive(*at(unit, dx), WHOLE)
            add(*at(unit, dx))

    exchanged(0)
    send_to(0, A, 0)
    own_part(A)
    exchanged(1)
    send_to(0, B, 1)
    own_part(B)
    send_to(1, A, 0)
    send_to(2, A, 0)
    receive(0, A, 0)
    spread(U[0], A)
    send_to(1, B, 1)
    send_to(2, B, 1)
    receive(0, B, 1)
    spread(U[0], B)
    cross(U[0])
    send_to(3, A, 0)
    send_to(3, B, 1)
    added(U[0], 0)
    relay(U[0], A)
    for n in (1, 2):
        receive(n, A, 0)
        cross(U[n], 0, A)
        spread(U[n], A)
    relay(U[0], B)
    added(U[0], 3, 1)
    for n in (1, 2):
        receive(n, B, 1)
        cross(U[n], 0, B)
        spread(U[n], B)
        added(U[n], 0)
    for n in (2, 1):
        relay(U[n], A)
    for n in (2, 1):
        crossed(V[n], A)
    finish(U[0], A, B)
    for n in (2, 1):
        relay(U[n], B)
        added(U[n], 3, 1)
    receive(3, A, 0)
    cross(U[3], 0, A)
    spread(U[3], A)
    for n in (2, 1):
        crossed(V[n], B)
        added(V[n], 0)
    receive(3, B, 1)
    cross(U[3], 0, B)
    spread(U[3], B)
    added(U[3], 0)
    cross(U[0], 1)
    cross(U[0], 3)
    finish(U[2], A, B)
    cross(U[2], 2)
    cross(U[0], 2)
    finish(U[1], A, B)
    crossed(V[3], A)
    for n in (3, 1):
        for span in PARTS:
            arrive(*at(V[2], n), span)
        add(*at(V[2], n))
    relay(V[1], A)
    relay(V[1], B)
    added(V[1], 3, 1)
    crossed(V[3], B)
    added(V[3], 0)
    relay(U[3], A)
    relay(V[3], A)
    relay(U[3], B)
    added(U[3], 3, 1)
    relay(V[3], B)
    added(V[3], 3, 1)
    take(V[2], 2)
    finish(V[1], A, B)
    take(V[0], 0, 1)
    finish(U[3], A, B)
    take(V[0], 3, 2)
    finish(V[3], A, B)
    for p in range(2):
        wait_for(s1[p].at[pl.ds(0, NL - 1)], s1_send.at[p])
    wait_for(s2, s2_send)
    wait_for(gat.at[pl.ds(0, NL - 1)], g_send)


FIRST = {0: 0, 2: SIDE - 1, 1: 2 * SIDE - 1, 3: 3 * SIDE - 1}


STORES = 8


def store(held, out, sem):
    size = held.shape[0] // STORES
    copies = []
    for n in range(STORES):
        rows = pl.ds(n * size, size)
        cp = pltpu.make_async_copy(held.at[rows], out.at[rows], sem.at[n])
        cp.start()
        copies.append(cp)
    for cp in copies:
        cp.wait()


def on_device(update, resident, placement, counts):
    _, rows, cols = resident.shape
    bf16 = jnp.bfloat16
    dma = pltpu.SemaphoreType.DMA
    result = pl.pallas_call(
        kernel,
        out_shape=pltpu.VMEM((rows, cols), bf16),
        in_specs=[pl.BlockSpec(memory_space=pltpu.HBM)] * 4,
        out_specs=pl.BlockSpec(memory_space=pltpu.VMEM),
        scratch_shapes=[
            pltpu.VMEM((EXP, TPD, LANE, LANE), jnp.float32),
            pltpu.VMEM((rows, cols), bf16),
            *[pltpu.VMEM((NL, EXP, size, SLAB, LANE), bf16) for _ in range(2) for _, size in PARTS],
            pltpu.VMEM((NE - 1, TPD, SLAB, LANE), bf16),
            pltpu.VMEM((NL, NH, SIDE, TPD, SLAB, LANE), bf16),
            pltpu.VMEM((1, NE), jnp.int32),
            pltpu.SMEM((NE,), jnp.int32),
            pltpu.VMEM((NE, LANE), jnp.int32),
            pltpu.SMEM((NE, LANE), jnp.int32),
            dma((5,)),
            dma((2,)),
            dma((2,)),
            dma,
            dma((2, 4)),
            dma,
            dma((NL, NH, 4)),
        ],
        compiler_params=pltpu.CompilerParams(collective_id=0, has_side_effects=True, vmem_limit_bytes=VMEM_LIMIT),
        name="refresh",
    )(*(pltpu.with_memory_space_constraint(a, pltpu.HBM) for a in (update, resident.reshape(rows, cols), placement.reshape(1, NE), counts)))
    final = pl.pallas_call(
        store,
        out_shape=pltpu.HBM((rows, cols), bf16),
        in_specs=[pl.BlockSpec(memory_space=pltpu.VMEM)],
        out_specs=pl.BlockSpec(memory_space=pltpu.HBM),
        scratch_shapes=[dma((STORES,))],
        compiler_params=pltpu.CompilerParams(vmem_limit_bytes=16 << 20),
        name="store",
    )(pltpu.with_memory_space_constraint(result, pltpu.VMEM))
    return final[None]


def solution(mesh):
    placed = (P("learn", "expert", None, None), P("expert", None, None), P(), P())
    return jax.shard_map(
        on_device, mesh=mesh, in_specs=placed, out_specs=P("expert", None, None), check_vma=False
    )
```
